32 devices in a mesh: dp: 4 (over x, core), seq: 2 (over y), tensor: 4 (over z).
Axes of the slice: x: 2, y: 2, z: 4, core: 2. Of those that a mesh axis runs over, the one named last changes fastest.
Arguments:
- lower: bfloat16 [2560, 4096], P(('dp', 'seq', 'tensor')), may hold values from -6 to 6
- upper: bfloat16 [2560, 4096], P(('dp', 'seq', 'tensor')), may hold values from -4 to 4
- grad_upper: bfloat16 [2560, 4096], P(('dp', 'seq', 'tensor')), may hold values from -6 to 6
- grad_lower: bfloat16 [2560, 4096], P(('dp', 'seq', 'tensor')), may hold values from -4 to 4
- positions: int32 [4, 640], P('dp'), may hold values from 0 to 399, as said below
- norm_gain: float32 [4096], replicated, may hold values from 0.1 to 1.9
- w_query: bfloat16 [4096, 4096], P(None, 'tensor'), may hold values from -1.875 to 1.875
- w_key: bfloat16 [4096, 1024], P(None, 'tensor'), may hold values from -0.09375 to 0.09375
- w_value: bfloat16 [4096, 1024], P(None, 'tensor'), may hold values from -0.09375 to 0.09375
- w_out: bfloat16 [4096, 4096], P('tensor'), may hold values from -0.375 to 0.375
Outputs:
- restored: bfloat16 [2560, 4096], P(('dp', 'seq', 'tensor'))
- grad_lower_in: bfloat16 [2560, 4096], P(('dp', 'seq', 'tensor'))
- grad_query: float32 [4096, 4096], P(('dp', 'seq'), 'tensor')
- grad_key: float32 [4096, 1024], P(('dp', 'seq'), 'tensor')
- grad_value: float32 [4096, 1024], P(('dp', 'seq'), 'tensor')
- grad_out: float32 [4096, 4096], P('tensor', ('dp', 'seq'))
The draws below stay inside these ranges and needn't reach their ends.
Inputs may be any that keep to these rules, and one draw needn't show every extreme that they name: `positions`: each group's row packs three documents in order; a position counts tokens from its document's start; the second document has exactly 400 tokens and starts before 3 * 80.
All inputs are finite; a program needn't handle non-finite values.
Results may differ from the reference program's by a relative error of at most 0.02.
The reference program's roundings to bfloat16 on the way count: a program that leaves them out, or rounds other values in their place, can miss the bound.
Values may be sent and summed in bfloat16 or wider, within the bound.
A program may use at most 192 MiB of HBM per device.

```python
import math
from functools import partial
import jax
import jax.numpy as jnp
from jax import lax

D = 4096
HEADS = 32
HD = 128
KVH = 8
SEQ_LEN = 640
GROUPS = 4
TOKENS = 2560
QW = 4096
KW = 1024
N_SEQ = 2
N_TENSOR = 4


def draw_positions(key, part):
    key = jax.random.fold_in(key, 5)
    starts = jax.random.randint(key, (GROUPS, 1), 1, 3 * SEQ_LEN // 8)
    second = 5 * SEQ_LEN // 8
    steps = jnp.arange(SEQ_LEN, dtype=jnp.int32)[None, :]
    inside = jnp.where(steps < starts + second, steps - starts, steps - starts - second)
    return jnp.where(steps < starts, steps, inside).astype(jnp.int32)


def draw_w_query(key, part):
    key = jax.random.fold_in(key, 11)
    first_key = jax.random.fold_in(key, 0)
    values = jax.random.truncated_normal(first_key, -3.0, 3.0, (D, HEADS * HD), jnp.float32) / math.sqrt(D)
    return values.astype(jnp.bfloat16)


def level_of(own_key, shape, cuts, low, high):
    level, own = 1.0, jax.random.fold_in(own_key, 6)
    for dim, blocks in cuts:
        draws = jnp.exp(jax.random.uniform(jax.random.fold_in(own, dim), (blocks,), jnp.float32, low / len(cuts), high / len(cuts)))
        level = level * jnp.repeat(draws, shape[dim] // blocks).reshape([-1 if axis == dim else 1 for axis in range(len(shape))])
    return level


def noise(rng, dims, deviation, limit, pieces=(), kind=jnp.bfloat16):
    entries = jax.random.normal(rng, dims, jnp.float32) * deviation
    if len(pieces) > 0:
        entries = level_of(rng, dims, pieces, -0.22, 0.18) * entries
    return jnp.clip(entries, min=-limit, max=limit).astype(kind)


def setup_inputs(seed: int = 0) -> dict:
    arg_keys = jax.random.split(jax.random.key(seed), 11)
    return {
        "lower": noise(arg_keys[0], (TOKENS, D), 1.0, 6.0, ((0, 32),)),
        "upper": noise(arg_keys[1], (TOKENS, D), 0.5, 4.0, ((0, 32),)),
        "grad_upper": noise(arg_keys[2], (TOKENS, D), 1.0, 6.0, ((0, 32),)),
        "grad_lower": noise(arg_keys[3], (TOKENS, D), 0.5, 4.0, ((0, 32),)),
        "positions": draw_positions(jax.random.fold_in(arg_keys[10], 71), 0),
        "norm_gain": jnp.clip(1.0 + 0.18 * jax.random.normal(arg_keys[5], (D,), jnp.float32), 0.1, 1.9),
        "w_query": draw_w_query(jax.random.fold_in(arg_keys[10], 71), 0),
        "w_key": noise(arg_keys[7], (D, KW), D ** -0.5, 0.09375, ((1, 4),)),
        "w_value": noise(arg_keys[8], (D, KW), D ** -0.5, 0.09375, ((1, 4),)),
        "w_out": noise(arg_keys[9], (QW, D), (QW // 16) ** -0.5, 0.375, ((0, 4),)),
    }


def tables(positions_row):
    half = HD // 2
    freq = jnp.exp(jnp.arange(half, dtype=jnp.float32) * (-2.0 * math.log(10000.0) / HD))
    angle = positions_row.astype(jnp.float32)[:, None] * freq[None, :]
    return (jnp.cos(angle), jnp.sin(angle))

def rotate(values, cosine, sine):
    half = values.shape[-1] // 2
    first = values[..., :half]
    second = values[..., half:]
    cosine = cosine[:, None, :]
    sine = sine[:, None, :]
    return jnp.concatenate([first * cosine - second * sine, second * cosine + first * sine], -1)

def unrotate(values, cosine, sine):
    half = values.shape[-1] // 2
    first = values[..., :half]
    second = values[..., half:]
    cosine = cosine[:, None, :]
    sine = sine[:, None, :]
    return jnp.concatenate([first * cosine + second * sine, second * cosine - first * sine], -1)

def rounded(values):
    return lax.optimization_barrier(values.astype(jnp.bfloat16)).astype(jnp.float32)

def one_group(norm_gain, weights, carry, inputs):
    lower_rows, upper_rows, dup_rows, dlow_rows, group_positions = inputs
    grad_q_acc, grad_k_acc, grad_v_acc, grad_o_acc = carry
    half_rows = SEQ_LEN // N_SEQ
    head_local = HEADS // N_TENSOR
    kv_local = KVH // N_TENSOR
    q_width = head_local * HD
    k_width = kv_local * HD
    scale = HD ** (-0.5)
    lower_f = lower_rows.astype(jnp.float32)
    inverse = lax.rsqrt(lax.optimization_barrier(jnp.mean(lower_f * lower_f, -1, keepdims=True)) + 1e-05)
    normed = lower_f * inverse
    hidden = (normed * norm_gain).astype(jnp.bfloat16)
    cosine, sine = tables(group_positions)
    steps = jnp.arange(SEQ_LEN, dtype=jnp.int32)
    offset = steps[:, None] - steps[None, :]
    allowed = (offset >= 0) & (offset <= group_positions[:, None])
    mixed = [jnp.zeros((half_rows, D), jnp.float32) for half_idx in range(N_SEQ)]
    grad_hidden = [jnp.zeros((half_rows, D), jnp.float32) for half_idx in range(N_SEQ)]
    hidden_f = hidden.astype(jnp.float32)
    for shard in range(N_TENSOR):
        w_query_s = weights[0][:, shard * q_width:(shard + 1) * q_width]
        w_key_s = weights[1][:, shard * k_width:(shard + 1) * k_width]
        w_value_s = weights[2][:, shard * k_width:(shard + 1) * k_width]
        w_out_s = weights[3][shard * q_width:(shard + 1) * q_width, :]
        keys = jnp.dot(hidden, w_key_s, preferred_element_type=jnp.float32).reshape(SEQ_LEN, kv_local, HD)
        keys = rotate(keys, cosine, sine).astype(jnp.bfloat16).reshape(SEQ_LEN, k_width)
        values = jnp.dot(hidden, w_value_s, preferred_element_type=jnp.float32).astype(jnp.bfloat16)
        keys_f = keys.astype(jnp.float32).reshape(SEQ_LEN, kv_local, HD)
        values_f = values.astype(jnp.float32).reshape(SEQ_LEN, kv_local, HD)
        key_sum = jnp.zeros((SEQ_LEN, k_width), jnp.float32)
        value_sum = jnp.zeros((SEQ_LEN, k_width), jnp.float32)
        saved = []
        for half_idx in range(N_SEQ):
            start = half_idx * half_rows
            hidden_s = hidden[start:start + half_rows]
            cos_s = cosine[start:start + half_rows]
            sin_s = sine[start:start + half_rows]
            queries = jnp.dot(hidden_s, w_query_s, preferred_element_type=jnp.float32).reshape(half_rows, head_local, HD)
            queries = rotate(queries, cos_s, sin_s).astype(jnp.bfloat16)
            queries_f = queries.astype(jnp.float32).reshape(half_rows, kv_local, -1, HD)
            scores = jnp.einsum('rkgd,lkd->kgrl', queries_f, keys_f) * scale
            scores = jnp.where(allowed[start:start + half_rows][None, None], scores, -1e+30)
            top = lax.optimization_barrier(jnp.max(scores, -1, keepdims=True))
            weights_e = jnp.exp(scores - top)
            probs = weights_e / lax.optimization_barrier(jnp.sum(weights_e, -1, keepdims=True))
            probs_b = probs.astype(jnp.bfloat16)
            probs_bf = probs_b.astype(jnp.float32)
            attn = jnp.einsum('kgrl,lkd->rkgd', probs_bf, values_f).astype(jnp.bfloat16).reshape(half_rows, q_width)
            mixed[half_idx] = mixed[half_idx] + rounded(jnp.dot(attn, w_out_s, preferred_element_type=jnp.float32))
            dup_s = dup_rows[start:start + half_rows]
            grad_attn = lax.dot_general(dup_s, w_out_s, (((1,), (1,)), ((), ())), preferred_element_type=jnp.float32).astype(jnp.bfloat16)
            term_out = lax.dot_general(attn, dup_s, (((0,), (0,)), ((), ())), preferred_element_type=jnp.float32)
            grad_o_acc = grad_o_acc.at[shard * q_width:(shard + 1) * q_width, :].add(rounded(term_out))
            grad_f = grad_attn.astype(jnp.float32).reshape(half_rows, kv_local, -1, HD)
            grad_probs = jnp.einsum('rkgd,lkd->kgrl', grad_f, values_f)
            delta = lax.optimization_barrier(jnp.sum(probs * grad_probs, -1, keepdims=True))
            grad_scores = (probs * (grad_probs - delta) * scale).astype(jnp.bfloat16).astype(jnp.float32)
            grad_q = jnp.einsum('kgrl,lkd->rkgd', grad_scores, keys_f).reshape(half_rows, head_local, HD)
            key_sum = key_sum + jnp.einsum('kgrl,rkgd->lkd', grad_scores, queries_f).reshape(SEQ_LEN, k_width)
            value_sum = value_sum + jnp.einsum('kgrl,rkgd->lkd', probs_bf, grad_f).reshape(SEQ_LEN, k_width)
            saved.append(grad_q)
        for half_idx in range(N_SEQ):
            start = half_idx * half_rows
            cos_s = cosine[start:start + half_rows]
            sin_s = sine[start:start + half_rows]
            grad_query_rows = unrotate(saved[half_idx], cos_s, sin_s).astype(jnp.bfloat16).reshape(half_rows, q_width)
            grad_key_rows = unrotate(key_sum[start:start + half_rows].reshape(half_rows, kv_local, HD), cos_s, sin_s).astype(jnp.bfloat16).reshape(half_rows, k_width)
            grad_value_rows = value_sum[start:start + half_rows].astype(jnp.bfloat16)
            hidden_sf = hidden_f[start:start + half_rows]
            grad_q_acc = grad_q_acc.at[:, shard * q_width:(shard + 1) * q_width].add(rounded(jnp.dot(hidden_sf.T, grad_query_rows.astype(jnp.float32))))
            grad_k_acc = grad_k_acc.at[:, shard * k_width:(shard + 1) * k_width].add(rounded(jnp.dot(hidden_sf.T, grad_key_rows.astype(jnp.float32))))
            grad_v_acc = grad_v_acc.at[:, shard * k_width:(shard + 1) * k_width].add(rounded(jnp.dot(hidden_sf.T, grad_value_rows.astype(jnp.float32))))
            term = lax.dot_general(grad_query_rows, w_query_s, (((1,), (1,)), ((), ())), preferred_element_type=jnp.float32)
            term = term + lax.dot_general(grad_key_rows, w_key_s, (((1,), (1,)), ((), ())), preferred_element_type=jnp.float32)
            term = term + lax.dot_general(grad_value_rows, w_value_s, (((1,), (1,)), ((), ())), preferred_element_type=jnp.float32)
            grad_hidden[half_idx] = grad_hidden[half_idx] + rounded(term)
    mixed_all = jnp.concatenate(mixed, 0)
    grad_all = jnp.concatenate(grad_hidden, 0)
    restored = (upper_rows.astype(jnp.float32) - mixed_all).astype(jnp.bfloat16)
    scaled = norm_gain * grad_all
    grad_in = inverse * (scaled - normed * lax.optimization_barrier(jnp.mean(scaled * normed, -1, keepdims=True)))
    grad_in = (dlow_rows.astype(jnp.float32) + grad_in).astype(jnp.bfloat16)
    return ((grad_q_acc, grad_k_acc, grad_v_acc, grad_o_acc), (restored, grad_in))

def reference(lower, upper, grad_upper, grad_lower, positions, norm_gain, w_query, w_key, w_value, w_out):
    shape_rows = (GROUPS, SEQ_LEN, D)
    inputs = (lower.reshape(shape_rows), upper.reshape(shape_rows), grad_upper.reshape(shape_rows), grad_lower.reshape(shape_rows), positions)
    carry = (jnp.zeros((D, QW), jnp.float32), jnp.zeros((D, KW), jnp.float32), jnp.zeros((D, KW), jnp.float32), jnp.zeros((QW, D), jnp.float32))
    stepper = partial(one_group, norm_gain, (w_query, w_key, w_value, w_out))
    carry, outputs = lax.scan(stepper, carry, inputs)
    restored = outputs[0].reshape(TOKENS, D)
    grad_in = outputs[1].reshape(TOKENS, D)
    return (restored, grad_in, carry[0], carry[1], carry[2], carry[3])
```

```python
import functools
import math

import jax
import jax.numpy as jnp
from jax import lax
from jax.experimental import pallas as pl
from jax.experimental.pallas import tpu as pltpu
from jax.sharding import PartitionSpec as P

HD = 128
F32 = jnp.float32
BF16 = jnp.bfloat16
VMEM_LIMIT = 40 * 1024 * 1024


def tables(positions):
    half = HD // 2
    freq = jnp.exp(jnp.arange(half, dtype=F32) * (-2.0 * math.log(10000.0) / HD))
    angle = positions.astype(F32)[:, None] * freq[None, :]
    cosine, sine = jnp.cos(angle), jnp.sin(angle)
    return jnp.concatenate([cosine, cosine], -1), jnp.concatenate([-sine, sine], -1)


def norm_rows(rows_in, norm_gain):
    rows_f = rows_in.astype(F32)
    inverse = lax.rsqrt(jnp.mean(rows_f * rows_f, -1, keepdims=True) + 1e-05)
    normed = rows_f * inverse
    return (normed, inverse, (normed * norm_gain).astype(BF16))


def contract_last(left, right):
    return lax.dot_general(left, right, (((1,), (1,)), ((), ())), preferred_element_type=F32)


def contract_first(left, right):
    return lax.dot_general(left, right, (((0,), (0,)), ((), ())), preferred_element_type=F32)


def turn(values, cosine, sine):
    return values * cosine + pltpu.roll(values, HD // 2, 1) * sine


def forward_body(q_ref, k_ref, v_ref, cos_ref, sin_ref, qi_ref, ki_ref, pos_ref, rot_ref, probs_ref, attn_ref):
    query = turn(q_ref[...], cos_ref[...], sin_ref[...]).astype(BF16)
    rot_ref[...] = query
    scores = contract_last(query, k_ref[...]) * (HD ** (-0.5))
    offset = qi_ref[...] - ki_ref[...]
    allowed = (offset >= 0) & (offset <= pos_ref[...])
    scores = jnp.where(allowed, scores, -1e30)
    weights = jnp.exp(scores - jnp.max(scores, -1, keepdims=True))
    probs = weights / jnp.sum(weights, -1, keepdims=True)
    probs_ref[0] = probs
    attn_ref[...] = jnp.dot(probs.astype(BF16), v_ref[...], preferred_element_type=F32).astype(BF16)


def backward_body(group, q_ref, k_ref, v_ref, cos_ref, sin_ref, probs_ref, g_ref, dq_ref, dk_ref, dv_ref):
    probs = probs_ref[0]
    grad = g_ref[...]
    grad_probs = contract_last(grad, v_ref[...])
    delta = jnp.sum(probs * grad_probs, -1, keepdims=True)
    grad_scores = (probs * (grad_probs - delta) * (HD ** (-0.5))).astype(BF16)
    grad_q = jnp.dot(grad_scores, k_ref[...], preferred_element_type=F32)
    dq_ref[...] = turn(grad_q, cos_ref[...], -sin_ref[...]).astype(BF16)
    dk = contract_first(grad_scores, q_ref[...])
    dv = contract_first(probs.astype(BF16), grad)
    first = lax.rem(pl.program_id(0), group) == 0

    @pl.when(first)
    def _():
        dk_ref[...] = dk
        dv_ref[...] = dv

    @pl.when(jnp.logical_not(first))
    def _():
        dk_ref[...] += dk
        dv_ref[...] += dv


def attention_specs(rows, length, group):
    head = pl.BlockSpec((rows, HD), lambda h: (0, h))
    shared = pl.BlockSpec((length, HD), lambda h: (0, h // group))
    table = pl.BlockSpec((rows, HD), lambda h: (0, 0))
    column = pl.BlockSpec((rows, 1), lambda h: (0, 0))
    line = pl.BlockSpec((1, length), lambda h: (0, 0))
    square = pl.BlockSpec((1, rows, length), lambda h: (h, 0, 0))
    return head, shared, table, column, line, square


def attention_forward(queries, keys, values, cosine, sine, query_idx, key_idx, positions):
    rows, width = queries.shape
    length = keys.shape[0]
    heads = width // HD
    head, shared, table, column, line, square = attention_specs(rows, length, width // keys.shape[1])
    pairs = heads * rows * length
    return pl.pallas_call(
        forward_body,
        grid=(heads,),
        in_specs=[head, shared, shared, table, table, column, line, column],
        out_specs=[head, square, head],
        out_shape=[
            jax.ShapeDtypeStruct((rows, width), BF16),
            jax.ShapeDtypeStruct((heads, rows, length), F32),
            jax.ShapeDtypeStruct((rows, width), BF16),
        ],
        compiler_params=pltpu.CompilerParams(vmem_limit_bytes=VMEM_LIMIT),
        cost_estimate=pl.CostEstimate(flops=4 * pairs * HD, bytes_accessed=4 * pairs, transcendentals=pairs),
        name="attention_forward",
    )(queries, keys, values, cosine, sine, query_idx[:, None], key_idx[None, :], positions[:, None])


def attention_backward(queries, keys, values, cosine, sine, probs, grads):
    rows, width = queries.shape
    length = keys.shape[0]
    heads = width // HD
    group = width // keys.shape[1]
    head, shared, table, column, line, square = attention_specs(rows, length, group)
    pairs = heads * rows * length
    return pl.pallas_call(
        functools.partial(backward_body, group),
        grid=(heads,),
        in_specs=[head, shared, shared, table, table, square, head],
        out_specs=[head, shared, shared],
        out_shape=[
            jax.ShapeDtypeStruct((rows, width), BF16),
            jax.ShapeDtypeStruct(keys.shape, F32),
            jax.ShapeDtypeStruct(keys.shape, F32),
        ],
        compiler_params=pltpu.CompilerParams(vmem_limit_bytes=VMEM_LIMIT),
        cost_estimate=pl.CostEstimate(flops=8 * pairs * HD, bytes_accessed=4 * pairs, transcendentals=0),
        name="attention_backward",
    )(queries, keys, values, cosine, sine, probs, grads)


def gather_cyclic(block):
    n = lax.axis_size("tensor")
    return [block] + [
        lax.ppermute(block, "tensor", [(i, (i + s) % n) for i in range(n)]) for s in range(1, n)
    ]


def scatter_cyclic(term, rows):
    n = lax.axis_size("tensor")
    total = term[:rows].astype(F32)
    for s in range(1, n):
        part = term[s * rows : (s + 1) * rows]
        total += lax.ppermute(part, "tensor", [(i, (i - s) % n) for i in range(n)]).astype(F32)
    return total


def scatter_groups(term):
    n_dp, n_seq = lax.axis_size("dp"), lax.axis_size("seq")
    dp, seq = lax.axis_index("dp"), lax.axis_index("seq")
    n = n_dp * n_seq
    rows, columns = term.shape[0] // n, term.shape[1]
    blocks = term.reshape(n_dp // 2, 2, n_seq * rows, columns)
    core = dp % 2
    send = lax.dynamic_index_in_dim(blocks, 1 - core, 1, keepdims=False)
    keep = lax.dynamic_index_in_dim(blocks, core, 1, keepdims=False)
    came = lax.ppermute(send, "dp", [(i, i ^ 1) for i in range(n_dp)])
    pair = (keep.astype(F32) + came.astype(F32)).astype(BF16)
    pair = pair.reshape(n // 2, rows, columns)
    mine = (dp // 2) * n_seq + seq
    total = lax.dynamic_index_in_dim(pair, mine, 0, keepdims=False).astype(F32)

    def partner(i, d):
        d_dp, d_seq = d // n_seq, d % n_seq
        i_dp, i_seq = i // n_seq, i % n_seq
        return (i_dp ^ (2 * d_dp)) * n_seq + (i_seq ^ d_seq)

    for d in range(n // 2 - 1, 0, -1):
        part = lax.dynamic_index_in_dim(pair, mine ^ d, 0, keepdims=False)
        total += lax.ppermute(part, ("dp", "seq"), [(i, partner(i, d)) for i in range(n)]).astype(F32)
    return total


def shards(
    lower, upper, grad_upper, grad_lower, positions, norm_gain, w_query, w_key, w_value, w_out
):
    rows = lower.shape[0]
    n_tensor = lax.axis_size("tensor")
    n_seq = lax.axis_size("seq")
    half_rows = rows * n_tensor
    k_width = w_key.shape[1]
    me_t = lax.axis_index("tensor")
    me_s = lax.axis_index("seq")

    lower_blocks = gather_cyclic(lower)
    upstream_blocks = gather_cyclic(grad_upper)

    local = jnp.concatenate(
        [((me_t - s) % n_tensor) * rows + jnp.arange(rows, dtype=jnp.int32) for s in range(n_tensor)]
    )
    own_idx = me_s * half_rows + local
    key_idx = jnp.concatenate([((me_s + e) % n_seq) * half_rows + local for e in range(n_seq)])
    own_pos = jnp.concatenate(
        [
            lax.dynamic_slice_in_dim(
                positions[0], me_s * half_rows + ((me_t - s) % n_tensor) * rows, rows, 0
            )
            for s in range(n_tensor)
        ]
    )
    cosine, sine = tables(own_pos)

    parts = [norm_rows(block, norm_gain) for block in lower_blocks]
    normed_own, inverse_own, _ = parts[0]
    hidden = jnp.concatenate([part[2] for part in parts], 0)

    def rope(values, sine_t):
        heads = values.reshape(half_rows, -1, HD)
        turned = jnp.concatenate([heads[..., HD // 2 :], heads[..., : HD // 2]], -1)
        return (heads * cosine[:, None, :] + turned * sine_t[:, None, :]).reshape(half_rows, -1)

    keys = rope(jnp.dot(hidden, w_key, preferred_element_type=F32), sine).astype(BF16)
    values = jnp.dot(hidden, w_value, preferred_element_type=F32).astype(BF16)
    both = jnp.concatenate([keys, values], 1)
    ring = [both]
    for e in range(1, n_seq):
        ring.append(lax.ppermute(both, "seq", [(i, (i - e) % n_seq) for i in range(n_seq)]))
    ring = jnp.concatenate(ring, 0)
    keys_all, values_all = ring[:, :k_width], ring[:, k_width:]
    queries = jnp.dot(hidden, w_query, preferred_element_type=F32)
    query_rot, probs, attn = attention_forward(
        queries, keys_all, values_all, cosine, sine, own_idx, key_idx, own_pos
    )
    mixed_term = jnp.dot(attn, w_out, preferred_element_type=F32).astype(BF16)
    mixed = scatter_cyclic(mixed_term, rows)
    restored = (upper.astype(F32) - mixed).astype(BF16)

    upstream = jnp.concatenate(upstream_blocks, 0)
    out_term = contract_first(upstream, attn).astype(BF16)
    grad_out = scatter_groups(out_term).T
    grad_attn = contract_last(upstream, w_out).astype(BF16)
    dq, key_terms, value_terms = attention_backward(
        query_rot, keys_all, values_all, cosine, sine, probs, grad_attn
    )
    terms = jnp.concatenate([key_terms, value_terms], 1)
    total = terms[:half_rows]
    for e in range(1, n_seq):
        part = terms[e * half_rows : (e + 1) * half_rows].astype(BF16)
        total += lax.ppermute(part, "seq", [(i, (i + e) % n_seq) for i in range(n_seq)]).astype(F32)
    dk = rope(total[:, :k_width], -sine).astype(BF16)
    dv = total[:, k_width:].astype(BF16)

    query_term = contract_first(hidden, dq).astype(BF16)
    grad_query = scatter_groups(query_term)
    kv_term = contract_first(hidden, jnp.concatenate([dk, dv], 1)).astype(BF16)
    grad_kv = scatter_groups(kv_term)
    grad_key, grad_value = grad_kv[:, :k_width], grad_kv[:, k_width:]

    hidden_term = contract_last(dq, w_query) + contract_last(dk, w_key) + contract_last(dv, w_value)
    grad_hidden = scatter_cyclic(hidden_term.astype(BF16), rows)
    scaled = norm_gain * grad_hidden
    grad_in = inverse_own * (scaled - normed_own * jnp.mean(scaled * normed_own, -1, keepdims=True))
    grad_lower_in = (grad_lower.astype(F32) + grad_in).astype(BF16)
    return (restored, grad_lower_in, grad_query, grad_key, grad_value, grad_out)


def solution(mesh):
    in_specs = (
        P(("dp", "seq", "tensor"), None),
        P(("dp", "seq", "tensor"), None),
        P(("dp", "seq", "tensor"), None),
        P(("dp", "seq", "tensor"), None),
        P("dp", None),
        P(),
        P(None, "tensor"),
        P(None, "tensor"),
        P(None, "tensor"),
        P("tensor", None),
    )
    out_specs = (
        P(("dp", "seq", "tensor"), None),
        P(("dp", "seq", "tensor"), None),
        P(("dp", "seq"), "tensor"),
        P(("dp", "seq"), "tensor"),
        P(("dp", "seq"), "tensor"),
        P("tensor", ("dp", "seq")),
    )
    return jax.shard_map(shards, mesh=mesh, in_specs=in_specs, out_specs=out_specs, check_vma=False)
```

```python
import functools
import math

import jax
import jax.numpy as jnp
from jax import lax
from jax.experimental import pallas as pl
from jax.experimental.pallas import tpu as pltpu
from jax.sharding import PartitionSpec as P

HD = 128
F32 = jnp.float32
BF16 = jnp.bfloat16
VMEM_LIMIT = 40 * 1024 * 1024


def tables(positions):
    half = HD // 2
    freq = jnp.exp(jnp.arange(half, dtype=F32) * (-2.0 * math.log(10000.0) / HD))
    angle = positions.astype(F32)[:, None] * freq[None, :]
    cosine, sine = jnp.cos(angle), jnp.sin(angle)
    return jnp.concatenate([cosine, cosine], -1), jnp.concatenate([-sine, sine], -1)


def norm_rows(rows_in, norm_gain):
    rows_f = rows_in.astype(F32)
    inverse = lax.rsqrt(jnp.mean(rows_f * rows_f, -1, keepdims=True) + 1e-05)
    normed = rows_f * inverse
    return (normed, inverse, (normed * norm_gain).astype(BF16))


def contract_last(left, right):
    return lax.dot_general(left, right, (((1,), (1,)), ((), ())), preferred_element_type=F32)


def contract_first(left, right):
    return lax.dot_general(left, right, (((0,), (0,)), ((), ())), preferred_element_type=F32)


def turn(values, cosine, sine):
    return values * cosine + pltpu.roll(values, HD // 2, 1) * sine


def forward_body(q_ref, k_ref, v_ref, cos_ref, sin_ref, qi_ref, ki_ref, pos_ref, rot_ref, probs_ref, attn_ref):
    query = turn(q_ref[...], cos_ref[...], sin_ref[...]).astype(BF16)
    rot_ref[...] = query
    scores = contract_last(query, k_ref[...]) * (HD ** (-0.5))
    offset = qi_ref[...] - ki_ref[...]
    allowed = (offset >= 0) & (offset <= pos_ref[...])
    scores = jnp.where(allowed, scores, -1e30)
    weights = jnp.exp(scores - jnp.max(scores, -1, keepdims=True))
    probs = weights / jnp.sum(weights, -1, keepdims=True)
    probs_ref[0] = probs
    attn_ref[...] = jnp.dot(probs.astype(BF16), v_ref[...], preferred_element_type=F32).astype(BF16)


def backward_body(group, q_ref, k_ref, v_ref, cos_ref, sin_ref, probs_ref, g_ref, dq_ref, dk_ref, dv_ref):
    probs = probs_ref[0]
    grad = g_ref[...]
    grad_probs = contract_last(grad, v_ref[...])
    delta = jnp.sum(probs * grad_probs, -1, keepdims=True)
    grad_scores = (probs * (grad_probs - delta) * (HD ** (-0.5))).astype(BF16)
    grad_q = jnp.dot(grad_scores, k_ref[...], preferred_element_type=F32)
    dq_ref[...] = turn(grad_q, cos_ref[...], -sin_ref[...]).astype(BF16)
    dk = contract_first(grad_scores, q_ref[...])
    dv = contract_first(probs.astype(BF16), grad)
    first = lax.rem(pl.program_id(0), group) == 0

    @pl.when(first)
    def _():
        dk_ref[...] = dk
        dv_ref[...] = dv

    @pl.when(jnp.logical_not(first))
    def _():
        dk_ref[...] += dk
        dv_ref[...] += dv


def attention_specs(rows, length, group):
    head = pl.BlockSpec((rows, HD), lambda h: (0, h))
    shared = pl.BlockSpec((length, HD), lambda h: (0, h // group))
    table = pl.BlockSpec((rows, HD), lambda h: (0, 0))
    column = pl.BlockSpec((rows, 1), lambda h: (0, 0))
    line = pl.BlockSpec((1, length), lambda h: (0, 0))
    square = pl.BlockSpec((1, rows, length), lambda h: (h, 0, 0))
    return head, shared, table, column, line, square


def attention_forward(queries, keys, values, cosine, sine, query_idx, key_idx, positions):
    rows, width = queries.shape
    length = keys.shape[0]
    heads = width // HD
    head, shared, table, column, line, square = attention_specs(rows, length, width // keys.shape[1])
    pairs = heads * rows * length
    return pl.pallas_call(
        forward_body,
        grid=(heads,),
        in_specs=[head, shared, shared, table, table, column, line, column],
        out_specs=[head, square, head],
        out_shape=[
            jax.ShapeDtypeStruct((rows, width), BF16),
            jax.ShapeDtypeStruct((heads, rows, length), F32),
            jax.ShapeDtypeStruct((rows, width), BF16),
        ],
        compiler_params=pltpu.CompilerParams(vmem_limit_bytes=VMEM_LIMIT),
        cost_estimate=pl.CostEstimate(flops=4 * pairs * HD, bytes_accessed=4 * pairs, transcendentals=pairs),
        name="attention_forward",
    )(queries, keys, values, cosine, sine, query_idx[:, None], key_idx[None, :], positions[:, None])


def attention_backward(queries, keys, values, cosine, sine, probs, grads):
    rows, width = queries.shape
    length = keys.shape[0]
    heads = width // HD
    group = width // keys.shape[1]
    head, shared, table, column, line, square = attention_specs(rows, length, group)
    pairs = heads * rows * length
    return pl.pallas_call(
        functools.partial(backward_body, group),
        grid=(heads,),
        in_specs=[head, shared, shared, table, table, square, head],
        out_specs=[head, shared, shared],
        out_shape=[
            jax.ShapeDtypeStruct((rows, width), BF16),
            jax.ShapeDtypeStruct(keys.shape, F32),
            jax.ShapeDtypeStruct(keys.shape, F32),
        ],
        compiler_params=pltpu.CompilerParams(vmem_limit_bytes=VMEM_LIMIT),
        cost_estimate=pl.CostEstimate(flops=8 * pairs * HD, bytes_accessed=4 * pairs, transcendentals=0),
        name="attention_backward",
    )(queries, keys, values, cosine, sine, probs, grads)


def after(value, *others):
    return lax.optimization_barrier((value,) + others)[0]


def gather_half(block):
    return lax.all_gather(block, "tensor", axis=0, tiled=True)


def scatter_half(term):
    return lax.psum_scatter(term, "tensor", scatter_dimension=0, tiled=True)


def group_blocks(term):
    n_dp, n_seq = lax.axis_size("dp"), lax.axis_size("seq")
    return term.reshape(n_dp // 2, 2, n_seq * term.shape[0] // (n_dp * n_seq), term.shape[1])


def core_exchange(term):
    n_dp = lax.axis_size("dp")
    core = lax.axis_index("dp") % 2
    send = lax.dynamic_index_in_dim(group_blocks(term), 1 - core, 1, keepdims=False)
    return lax.ppermute(send, "dp", [(i, i ^ 1) for i in range(n_dp)])


def core_sum(term, came):
    n_dp, n_seq = lax.axis_size("dp"), lax.axis_size("seq")
    core = lax.axis_index("dp") % 2
    keep = lax.dynamic_index_in_dim(group_blocks(term), core, 1, keepdims=False)
    pair = (keep.astype(F32) + came.astype(F32)).astype(BF16)
    n = n_dp * n_seq
    return pair.reshape(n // 2, term.shape[0] // n, term.shape[1])


def chip_exchange(pair):
    n_dp, n_seq = lax.axis_size("dp"), lax.axis_size("seq")
    n = n_dp * n_seq
    mine = (lax.axis_index("dp") // 2) * n_seq + lax.axis_index("seq")

    def partner(i, d):
        return ((i // n_seq) ^ (2 * (d // n_seq))) * n_seq + ((i % n_seq) ^ (d % n_seq))

    parts = [lax.dynamic_index_in_dim(pair, mine, 0, keepdims=False)]
    for d in range(n // 2 - 1, 0, -1):
        part = lax.dynamic_index_in_dim(pair, mine ^ d, 0, keepdims=False)
        parts.append(lax.ppermute(part, ("dp", "seq"), [(i, partner(i, d)) for i in range(n)]))
    return parts


def add_parts(parts):
    return functools.reduce(lambda total, part: total + part.astype(F32), parts[1:], parts[0].astype(F32))


def shards(
    lower, upper, grad_upper, grad_lower, positions, norm_gain, w_query, w_key, w_value, w_out
):
    half_rows = lower.shape[0] * lax.axis_size("tensor")
    n_seq = lax.axis_size("seq")
    k_width = w_key.shape[1]
    q_width = w_query.shape[1]
    me_s = lax.axis_index("seq")

    lower_rows = gather_half(lower)
    upstream = gather_half(after(grad_upper, lower_rows))

    local = jnp.arange(half_rows, dtype=jnp.int32)
    own_idx = me_s * half_rows + local
    key_idx = jnp.concatenate([((me_s + e) % n_seq) * half_rows + local for e in range(n_seq)])
    own_pos = lax.dynamic_slice_in_dim(positions[0], me_s * half_rows, half_rows, 0)
    cosine, sine = tables(own_pos)
    hidden = norm_rows(lower_rows, norm_gain)[2]

    def rope(values, sine_t):
        heads = values.reshape(half_rows, -1, HD)
        turned = jnp.concatenate([heads[..., HD // 2 :], heads[..., : HD // 2]], -1)
        return (heads * cosine[:, None, :] + turned * sine_t[:, None, :]).reshape(half_rows, -1)

    keys = rope(jnp.dot(hidden, w_key, preferred_element_type=F32), sine).astype(BF16)
    values = jnp.dot(hidden, w_value, preferred_element_type=F32).astype(BF16)
    both = jnp.concatenate([keys, values], 1)
    ring = [both]
    for e in range(1, n_seq):
        ring.append(lax.ppermute(both, "seq", [(i, (i - e) % n_seq) for i in range(n_seq)]))
    ring = jnp.concatenate(ring, 0)
    keys_all, values_all = ring[:, :k_width], ring[:, k_width:]
    queries = jnp.dot(hidden, w_query, preferred_element_type=F32)
    query_rot, probs, attn = attention_forward(
        queries, keys_all, values_all, cosine, sine, own_idx, key_idx, own_pos
    )
    mixed_term = jnp.dot(attn, w_out, preferred_element_type=F32).astype(BF16)
    upstream, mixed_term = lax.optimization_barrier((upstream, mixed_term))
    mixed = scatter_half(mixed_term)

    out_term = contract_first(upstream, attn).astype(BF16)
    out_came = core_exchange(out_term)
    grad_attn = contract_last(upstream, w_out).astype(BF16)
    dq, key_terms, value_terms = attention_backward(
        query_rot, keys_all, values_all, cosine, sine, probs, grad_attn
    )
    terms = jnp.concatenate([key_terms, value_terms], 1)
    total = terms[:half_rows]
    for e in range(1, n_seq):
        part = terms[e * half_rows : (e + 1) * half_rows].astype(BF16)
        total += lax.ppermute(part, "seq", [(i, (i + e) % n_seq) for i in range(n_seq)]).astype(F32)
    out_pair = core_sum(out_term, out_came)
    out_pair, total = lax.optimization_barrier((out_pair, total))
    out_parts = chip_exchange(out_pair)
    dk = rope(total[:, :k_width], -sine).astype(BF16)
    dv = total[:, k_width:].astype(BF16)

    grads = jnp.concatenate([dq, dk, dv], 1)
    weight_term = contract_first(hidden, after(grads, mixed, *out_parts[2:3])).astype(BF16)
    weight_came = core_exchange(weight_term)
    hidden_term = contract_last(after(dq, weight_term, *out_parts[1:]), w_query) + contract_last(dk, w_key) + contract_last(dv, w_value)
    grad_hidden = scatter_half(hidden_term.astype(BF16)).astype(F32)
    weight_pair = core_sum(weight_term, weight_came)
    weight_pair, out_parts = lax.optimization_barrier((weight_pair, out_parts))
    weight_parts = chip_exchange(weight_pair)

    grad_out = add_parts(out_parts).T
    restored = (upper.astype(F32) - mixed.astype(F32)).astype(BF16)
    normed, inverse, _ = norm_rows(lower, norm_gain)
    scaled = norm_gain * grad_hidden
    grad_in = inverse * (scaled - normed * jnp.mean(scaled * normed, -1, keepdims=True))
    grad_lower_in = (grad_lower.astype(F32) + grad_in).astype(BF16)
    grad_query = add_parts([part[:, :q_width] for part in weight_parts])
    grad_key = add_parts([part[:, q_width : q_width + k_width] for part in weight_parts])
    grad_value = add_parts([part[:, q_width + k_width :] for part in weight_parts])
    return (restored, grad_lower_in, grad_query, grad_key, grad_value, grad_out)


def solution(mesh):
    in_specs = (
        P(("dp", "seq", "tensor"), None),
        P(("dp", "seq", "tensor"), None),
        P(("dp", "seq", "tensor"), None),
        P(("dp", "seq", "tensor"), None),
        P("dp", None),
        P(),
        P(None, "tensor"),
        P(None, "tensor"),
        P(None, "tensor"),
        P("tensor", None),
    )
    out_specs = (
        P(("dp", "seq", "tensor"), None),
        P(("dp", "seq", "tensor"), None),
        P(("dp", "seq"), "tensor"),
        P(("dp", "seq"), "tensor"),
        P(("dp", "seq"), "tensor"),
        P("tensor", ("dp", "seq")),
    )
    return jax.shard_map(shards, mesh=mesh, in_specs=in_specs, out_specs=out_specs, check_vma=False)
```

```python
import functools
import math

import jax
import jax.numpy as jnp
from jax import lax
from jax.experimental import pallas as pl
from jax.experimental.pallas import tpu as pltpu
from jax.sharding import PartitionSpec as P

HD = 128
F32 = jnp.float32
BF16 = jnp.bfloat16
VMEM_LIMIT = 40 * 1024 * 1024


def tables(positions):
    half = HD // 2
    freq = jnp.exp(jnp.arange(half, dtype=F32) * (-2.0 * math.log(10000.0) / HD))
    angle = positions.astype(F32)[:, None] * freq[None, :]
    cosine, sine = jnp.cos(angle), jnp.sin(angle)
    return jnp.concatenate([cosine, cosine], -1), jnp.concatenate([-sine, sine], -1)


def norm_rows(rows_in, norm_gain):
    rows_f = rows_in.astype(F32)
    inverse = lax.rsqrt(jnp.mean(rows_f * rows_f, -1, keepdims=True) + 1e-05)
    normed = rows_f * inverse
    return (normed, inverse, (normed * norm_gain).astype(BF16))


def contract_last(left, right):
    return lax.dot_general(left, right, (((1,), (1,)), ((), ())), preferred_element_type=F32)


def contract_first(left, right):
    return lax.dot_general(left, right, (((0,), (0,)), ((), ())), preferred_element_type=F32)


def turn(values, cosine, sine):
    return values * cosine + pltpu.roll(values, HD // 2, 1) * sine


def forward_body(q_ref, k_ref, v_ref, cos_ref, sin_ref, qi_ref, ki_ref, pos_ref, rot_ref, probs_ref, attn_ref):
    query = turn(q_ref[...], cos_ref[...], sin_ref[...]).astype(BF16)
    rot_ref[...] = query
    scores = contract_last(query, k_ref[...]) * (HD ** (-0.5))
    offset = qi_ref[...] - ki_ref[...]
    allowed = (offset >= 0) & (offset <= pos_ref[...])
    scores = jnp.where(allowed, scores, -1e30)
    weights = jnp.exp(scores - jnp.max(scores, -1, keepdims=True))
    probs = weights / jnp.sum(weights, -1, keepdims=True)
    probs_ref[0] = probs
    attn_ref[...] = jnp.dot(probs.astype(BF16), v_ref[...], preferred_element_type=F32).astype(BF16)


def backward_body(group, q_ref, k_ref, v_ref, cos_ref, sin_ref, probs_ref, g_ref, dq_ref, dk_ref, dv_ref):
    probs = probs_ref[0]
    grad = g_ref[...]
    grad_probs = contract_last(grad, v_ref[...])
    delta = jnp.sum(probs * grad_probs, -1, keepdims=True)
    grad_scores = (probs * (grad_probs - delta) * (HD ** (-0.5))).astype(BF16)
    grad_q = jnp.dot(grad_scores, k_ref[...], preferred_element_type=F32)
    dq_ref[...] = turn(grad_q, cos_ref[...], -sin_ref[...]).astype(BF16)
    dk = contract_first(grad_scores, q_ref[...])
    dv = contract_first(probs.astype(BF16), grad)
    first = lax.rem(pl.program_id(0), group) == 0

    @pl.when(first)
    def _():
        dk_ref[...] = dk
        dv_ref[...] = dv

    @pl.when(jnp.logical_not(first))
    def _():
        dk_ref[...] += dk
        dv_ref[...] += dv


def attention_specs(rows, length, group):
    head = pl.BlockSpec((rows, HD), lambda h: (0, h))
    shared = pl.BlockSpec((length, HD), lambda h: (0, h // group))
    table = pl.BlockSpec((rows, HD), lambda h: (0, 0))
    column = pl.BlockSpec((rows, 1), lambda h: (0, 0))
    line = pl.BlockSpec((1, length), lambda h: (0, 0))
    square = pl.BlockSpec((1, rows, length), lambda h: (h, 0, 0))
    return head, shared, table, column, line, square


def attention_forward(queries, keys, values, cosine, sine, query_idx, key_idx, positions):
    rows, width = queries.shape
    length = keys.shape[0]
    heads = width // HD
    head, shared, table, column, line, square = attention_specs(rows, length, width // keys.shape[1])
    pairs = heads * rows * length
    return pl.pallas_call(
        forward_body,
        grid=(heads,),
        in_specs=[head, shared, shared, table, table, column, line, column],
        out_specs=[head, square, head],
        out_shape=[
            jax.ShapeDtypeStruct((rows, width), BF16),
            jax.ShapeDtypeStruct((heads, rows, length), F32),
            jax.ShapeDtypeStruct((rows, width), BF16),
        ],
        compiler_params=pltpu.CompilerParams(vmem_limit_bytes=VMEM_LIMIT),
        cost_estimate=pl.CostEstimate(flops=4 * pairs * HD, bytes_accessed=4 * pairs, transcendentals=pairs),
        name="attention_forward",
    )(queries, keys, values, cosine, sine, query_idx[:, None], key_idx[None, :], positions[:, None])


def attention_backward(queries, keys, values, cosine, sine, probs, grads):
    rows, width = queries.shape
    length = keys.shape[0]
    heads = width // HD
    group = width // keys.shape[1]
    head, shared, table, column, line, square = attention_specs(rows, length, group)
    pairs = heads * rows * length
    return pl.pallas_call(
        functools.partial(backward_body, group),
        grid=(heads,),
        in_specs=[head, shared, shared, table, table, square, head],
        out_specs=[head, shared, shared],
        out_shape=[
            jax.ShapeDtypeStruct((rows, width), BF16),
            jax.ShapeDtypeStruct(keys.shape, F32),
            jax.ShapeDtypeStruct(keys.shape, F32),
        ],
        compiler_params=pltpu.CompilerParams(vmem_limit_bytes=VMEM_LIMIT),
        cost_estimate=pl.CostEstimate(flops=8 * pairs * HD, bytes_accessed=4 * pairs, transcendentals=0),
        name="attention_backward",
    )(queries, keys, values, cosine, sine, probs, grads)


def after(value, *others):
    return lax.optimization_barrier((value,) + others)[0]


def gather_half(block):
    return lax.all_gather(block, "tensor", axis=0, tiled=True)


def scatter_half(term):
    return lax.psum_scatter(term, "tensor", scatter_dimension=0, tiled=True)


def group_blocks(term):
    n_dp, n_seq = lax.axis_size("dp"), lax.axis_size("seq")
    return term.reshape(n_dp // 2, 2, n_seq * term.shape[0] // (n_dp * n_seq), term.shape[1])


def core_exchange(term):
    n_dp = lax.axis_size("dp")
    core = lax.axis_index("dp") % 2
    send = lax.dynamic_index_in_dim(group_blocks(term), 1 - core, 1, keepdims=False)
    return lax.ppermute(send, "dp", [(i, i ^ 1) for i in range(n_dp)])


def chip_partner(i, d):
    n_seq = lax.axis_size("seq")
    return ((i // n_seq) ^ (2 * (d // n_seq))) * n_seq + ((i % n_seq) ^ (d % n_seq))


def pair_body(count, index_ref, *refs):
    for d in range(count):
        total = refs[d][...].astype(F32) + refs[count + d][...].astype(F32)
        refs[2 * count + d][...] = total[0].astype(BF16)


def core_sum(term, came):
    n_dp, n_seq = lax.axis_size("dp"), lax.axis_size("seq")
    n = n_dp * n_seq
    count, rows, columns = n // 2, term.shape[0] // n, term.shape[1]
    dp, seq = lax.axis_index("dp"), lax.axis_index("seq")
    me, mine = dp * n_seq + seq, (dp // 2) * n_seq + seq
    index = jnp.stack(
        [chip_partner(me, d) for d in range(count)] + [mine ^ d for d in range(count)]
    ).astype(jnp.int32)
    tile = math.gcd(128, rows)

    def at(place):
        return pl.BlockSpec((1, tile, columns), lambda t, index_ref: (index_ref[place], t, 0))

    return pl.pallas_call(
        functools.partial(pair_body, count),
        grid_spec=pltpu.PrefetchScalarGridSpec(
            num_scalar_prefetch=1,
            grid=(rows // tile,),
            in_specs=[at(place) for place in range(2 * count)],
            out_specs=[pl.BlockSpec((tile, columns), lambda t, index_ref: (t, 0))] * count,
        ),
        out_shape=[jax.ShapeDtypeStruct((rows, columns), BF16)] * count,
        compiler_params=pltpu.CompilerParams(vmem_limit_bytes=VMEM_LIMIT),
        cost_estimate=pl.CostEstimate(
            flops=count * rows * columns, bytes_accessed=6 * count * rows * columns, transcendentals=0
        ),
        name="core_sum",
    )(index, *[term.reshape(n, rows, columns)] * count, *[came.reshape(count, rows, columns)] * count)


def chip_exchange(pair):
    n = lax.axis_size("dp") * lax.axis_size("seq")
    parts = [pair[0]]
    for d in range(n // 2 - 1, 0, -1):
        ways = [(i, chip_partner(i, d)) for i in range(n)]
        parts.append(lax.ppermute(pair[d], ("dp", "seq"), ways))
    return parts


def turned_body(*refs):
    total = refs[0][...].astype(F32)
    for ref in refs[1:-1]:
        total += ref[...].astype(F32)
    refs[-1][...] = total.T


def add_turned(parts):
    rows, columns = parts[0].shape
    return pl.pallas_call(
        turned_body,
        grid=(columns // HD,),
        in_specs=[pl.BlockSpec((rows, HD), lambda c: (0, c))] * len(parts),
        out_specs=pl.BlockSpec((HD, rows), lambda c: (c, 0)),
        out_shape=jax.ShapeDtypeStruct((columns, rows), F32),
        compiler_params=pltpu.CompilerParams(vmem_limit_bytes=VMEM_LIMIT),
        name="add_turned",
    )(*parts)


def add_parts(parts):
    return functools.reduce(lambda total, part: total + part.astype(F32), parts[1:], parts[0].astype(F32))


def shards(
    lower, upper, grad_upper, grad_lower, positions, norm_gain, w_query, w_key, w_value, w_out
):
    half_rows = lower.shape[0] * lax.axis_size("tensor")
    n_seq = lax.axis_size("seq")
    k_width = w_key.shape[1]
    q_width = w_query.shape[1]
    me_s = lax.axis_index("seq")

    lower_rows = gather_half(lower)
    upstream = gather_half(after(grad_upper, lower_rows))

    local = jnp.arange(half_rows, dtype=jnp.int32)
    own_idx = me_s * half_rows + local
    key_idx = jnp.concatenate([((me_s + e) % n_seq) * half_rows + local for e in range(n_seq)])
    own_pos = lax.dynamic_slice_in_dim(positions[0], me_s * half_rows, half_rows, 0)
    cosine, sine = tables(own_pos)
    hidden = norm_rows(lower_rows, norm_gain)[2]

    def rope(values, sine_t):
        heads = values.reshape(half_rows, -1, HD)
        turned = jnp.concatenate([heads[..., HD // 2 :], heads[..., : HD // 2]], -1)
        return (heads * cosine[:, None, :] + turned * sine_t[:, None, :]).reshape(half_rows, -1)

    keys = rope(jnp.dot(hidden, w_key, preferred_element_type=F32), sine).astype(BF16)
    values = jnp.dot(hidden, w_value, preferred_element_type=F32).astype(BF16)
    both = jnp.concatenate([keys, values], 1)
    ring = [both]
    for e in range(1, n_seq):
        ring.append(lax.ppermute(both, "seq", [(i, (i - e) % n_seq) for i in range(n_seq)]))
    ring = jnp.concatenate(ring, 0)
    keys_all, values_all = ring[:, :k_width], ring[:, k_width:]
    queries = jnp.dot(hidden, w_query, preferred_element_type=F32)
    query_rot, probs, attn = attention_forward(
        queries, keys_all, values_all, cosine, sine, own_idx, key_idx, own_pos
    )
    mixed_term = jnp.dot(attn, w_out, preferred_element_type=F32).astype(BF16)
    upstream, mixed_term = lax.optimization_barrier((upstream, mixed_term))
    mixed = scatter_half(mixed_term)

    out_term = contract_first(upstream, attn).astype(BF16)
    out_came = core_exchange(out_term)
    grad_attn = contract_last(upstream, w_out).astype(BF16)
    dq, key_terms, value_terms = attention_backward(
        query_rot, keys_all, values_all, cosine, sine, probs, grad_attn
    )
    terms = jnp.concatenate([key_terms, value_terms], 1)
    total = terms[:half_rows]
    came = [
        lax.ppermute(
            terms[e * half_rows : (e + 1) * half_rows].astype(BF16),
            "seq",
            [(i, (i + e) % n_seq) for i in range(n_seq)],
        )
        for e in range(1, n_seq)
    ]
    out_pair = core_sum(out_term, out_came)
    came, out_pair = lax.optimization_barrier((came, out_pair))
    out_parts = chip_exchange(out_pair)
    total = add_parts([total] + came)
    dk = rope(total[:, :k_width], -sine).astype(BF16)
    dv = total[:, k_width:].astype(BF16)

    grads = jnp.concatenate([dq, dk, dv], 1)
    weight_term = contract_first(hidden, after(grads, mixed, *out_parts[2:])).astype(BF16)
    dq, dk, dv, weight_term = lax.optimization_barrier((dq, dk, dv, weight_term))
    weight_came = core_exchange(weight_term)
    hidden_term = contract_last(dq, w_query) + contract_last(after(dk, out_parts[1]), w_key) + contract_last(dv, w_value)
    hidden_term = hidden_term.astype(BF16)
    grad_hidden = scatter_half(hidden_term).astype(F32)
    weight_came = after(weight_came, hidden_term)
    weight_pair = core_sum(weight_term, weight_came)
    weight_pair, out_parts = lax.optimization_barrier((weight_pair, out_parts))
    weight_parts = chip_exchange(weight_pair)

    grad_out = add_turned(out_parts)
    restored = (upper.astype(F32) - mixed.astype(F32)).astype(BF16)
    normed, inverse, _ = norm_rows(lower, norm_gain)
    scaled = norm_gain * grad_hidden
    grad_in = inverse * (scaled - normed * jnp.mean(scaled * normed, -1, keepdims=True))
    grad_lower_in = (grad_lower.astype(F32) + grad_in).astype(BF16)
    grad_query = add_parts([part[:, :q_width] for part in weight_parts])
    grad_key = add_parts([part[:, q_width : q_width + k_width] for part in weight_parts])
    grad_value = add_parts([part[:, q_width + k_width :] for part in weight_parts])
    return (restored, grad_lower_in, grad_query, grad_key, grad_value, grad_out)


def solution(mesh):
    in_specs = (
        P(("dp", "seq", "tensor"), None),
        P(("dp", "seq", "tensor"), None),
        P(("dp", "seq", "tensor"), None),
        P(("dp", "seq", "tensor"), None),
        P("dp", None),
        P(),
        P(None, "tensor"),
        P(None, "tensor"),
        P(None, "tensor"),
        P("tensor", None),
    )
    out_specs = (
        P(("dp", "seq", "tensor"), None),
        P(("dp", "seq", "tensor"), None),
        P(("dp", "seq"), "tensor"),
        P(("dp", "seq"), "tensor"),
        P(("dp", "seq"), "tensor"),
        P("tensor", ("dp", "seq")),
    )
    return jax.shard_map(shards, mesh=mesh, in_specs=in_specs, out_specs=out_specs, check_vma=False)
```
